256 devices in a mesh: blk: 128 (over x, y_hi, z, core), rep: 2 (over y_lo).
Axes of the slice: x: 4, y: 4 (y_hi: 2, y_lo: 2; y = y_hi * 2 + y_lo), z: 8, core: 2. Of those that a mesh axis runs over, the one named last changes fastest.
Arguments:
- embeddings: bfloat16 [131072, 768], P('blk', 'rep'), as said below
- weights: bfloat16 [131072], P('blk'), may hold values from 0.25 to 4
Outputs:
- neighbours: bfloat16 [131072, 768], P('blk', 'rep')
- scores: float32 [131072], P('blk')
The draws below stay inside these ranges and needn't reach their ends.
Inputs may be any that keep to these rules, and one draw needn't show every extreme that they name: `embeddings`: finite values.
All inputs are finite; a program needn't handle non-finite values.
Results may differ from the reference program's by a relative error of at most 0.0034.
Values may be sent and summed in bfloat16 or wider, within the bound.
No kernel may reach another device: no remote copies, remote signals or barrier semaphores. Data moves between devices by JAX's collectives and lax.ppermute only.
A program may use at most 64 MiB of HBM per device.

```python
import math
import jax
import jax.numpy as jnp
from jax import lax

D = 768
ROWS = 1024
TOTAL = 131072
N_BLK = 128


def draw_embeddings(key, part):
    key = jax.random.fold_in(key, 7)
    total_rows = ROWS * N_BLK
    clusters = max(ROWS // 2, 4)
    centers = jax.random.normal(jax.random.fold_in(key, 2), (clusters, D), jnp.float32)
    members = jax.random.randint(jax.random.fold_in(key, 3), (total_rows,), 0, clusters)
    base = jax.random.normal(key, (total_rows, D), jnp.float32)
    strength = 2.5
    mixed = base + 0.7 * jnp.roll(base, ROWS, axis=0) + 0.7 * jnp.roll(base, 2 * ROWS, axis=0)
    mixed = mixed + strength * jnp.take(centers, members, axis=0)
    return mixed.astype(jnp.bfloat16)


def steps_of(rng, shape, split, smallest, top_value):
    def one(position, shards_of):
        heights = jax.random.uniform(jax.random.fold_in(jax.random.fold_in(rng, 6), position), (shards_of,), jnp.float32, smallest / len(split), top_value / len(split))
        return jnp.repeat(jnp.exp(heights), shape[position] // shards_of).reshape((-1,) + (1,) * (len(shape) - position - 1))

    level = one(*split[0])
    for cut in split[1:]:
        level = level * one(*cut)
    return level


def setup_inputs(seed: int = 0) -> dict:
    key_list = jax.random.split(jax.random.key(seed), 3)
    embeddings = draw_embeddings(jax.random.fold_in(key_list[2], 71), 0)
    weights = jnp.clip(jnp.exp(math.log(4.0) - 2.7725887 * jax.random.uniform(key_list[1], (TOTAL,), jnp.float32) ** steps_of(key_list[1], (TOTAL,), ((0, 128),), -0.2, 0.2)), 0.25, 4.0).astype(jnp.bfloat16)
    return {"embeddings": embeddings, "weights": weights}


sharpness = 12.0
epsilon = 1e-06

def prepare(embeddings, weights):
    values = embeddings.astype(jnp.float32)
    root_mean = jnp.sqrt(lax.optimization_barrier(jnp.mean(values * values, axis=1, keepdims=True)) + epsilon)
    scaled = values / root_mean
    unit_rows = scaled.astype(jnp.bfloat16)
    value_rows = (weights.astype(jnp.float32)[:, None] * scaled).astype(jnp.bfloat16)
    return (unit_rows, value_rows)

def kernel_of(queries, keys_unit):
    cosine = lax.dot_general(queries, keys_unit, (((1,), (1,)), ((), ())), preferred_element_type=jnp.float32)
    cosine = cosine / queries.shape[1]
    return jnp.exp(sharpness * (cosine - 1.0))

def reference(embeddings, weights):
    total_rows = embeddings.shape[0]
    unit_rows, value_rows = prepare(embeddings, weights)

    def one_slab(slab_index):
        start = slab_index * ROWS
        queries = lax.dynamic_slice_in_dim(unit_rows, start, ROWS, 0)
        key_index = (start - 2 * ROWS + jnp.arange(5 * ROWS, dtype=jnp.int32)) % total_rows
        keys_unit = jnp.take(unit_rows, key_index, axis=0)
        keys_value = jnp.take(value_rows, key_index, axis=0)
        keys_weight = jnp.take(weights, key_index, axis=0)
        query_index = start + jnp.arange(ROWS, dtype=jnp.int32)
        kernel = kernel_of(queries, keys_unit)
        kernel = jnp.where(query_index[:, None] == key_index[None, :], jnp.zeros_like(kernel), kernel)
        kernel = kernel.astype(jnp.bfloat16)
        row_sums = jnp.dot(kernel, keys_value, preferred_element_type=jnp.float32)
        masses = jnp.dot(kernel, keys_weight, preferred_element_type=jnp.float32)
        neighbours = (row_sums / masses[:, None]).astype(jnp.bfloat16)
        scores = jnp.log(masses) / sharpness + 1.0
        return (neighbours, scores)
    neighbours, scores = lax.map(one_slab, jnp.arange(N_BLK, dtype=jnp.int32))
    return (neighbours.reshape(total_rows, embeddings.shape[1]), scores.reshape(total_rows))
```

```python
import functools

import jax
import jax.numpy as jnp
from jax import lax
from jax.experimental import pallas as pl
from jax.experimental.pallas import tpu as pltpu
from jax.sharding import PartitionSpec as P

sharpness = 12.0
epsilon = 1e-06
LOG2E = 1.4426950408889634
QB = 256
WROWS = 16
RING = 16


def unit_scale(d0, d1):
    a = d0.astype(jnp.float32)
    b = d1.astype(jnp.float32)
    width = d0.shape[1] + d1.shape[1]
    total = jnp.sum(a * a, axis=1, keepdims=True) + jnp.sum(b * b, axis=1, keepdims=True)
    return a, b, lax.rsqrt(total / width + epsilon)


def log_weights(w_tile):
    logs = (jnp.log(w_tile.astype(jnp.float32)) - sharpness) * LOG2E
    return jnp.concatenate([logs[b : b + 1, :] for b in range(4)], axis=1)


def fill_keys(d0, d1, w_tile, flip, kn, bias):
    half = d0.shape[1]
    a, b, scale = unit_scale(d0, d1)
    first = pl.multiple_of(half - flip * half, half)
    second = pl.multiple_of(flip * half, half)
    kn[:, pl.ds(first, half)] = (a * scale).astype(jnp.bfloat16)
    kn[:, pl.ds(second, half)] = (b * scale).astype(jnp.bfloat16)
    kn[:, 2 * half :] = jnp.ones((kn.shape[0], kn.shape[1] - 2 * half), jnp.bfloat16)
    bias[...] = jnp.broadcast_to(log_weights(w_tile), bias.shape)


def add_slab(q, kn, bias, total, mask_from=None):
    half = kn.shape[1] // 7 * 3
    logits = lax.dot_general(
        q, kn[:, : 2 * half], (((1,), (1,)), ((), ())), preferred_element_type=jnp.float32
    )
    kernel = jnp.exp2(logits + bias[0:1, :])
    if mask_from is not None:
        rows = lax.broadcasted_iota(jnp.int32, kernel.shape, 0) + mask_from
        cols = lax.broadcasted_iota(jnp.int32, kernel.shape, 1)
        kernel = jnp.where(rows == cols, 0.0, kernel)
    return total + jnp.dot(
        kernel.astype(jnp.bfloat16), kn[:, half:], preferred_element_type=jnp.float32
    )


def first_kernel(e_ref, o_ref, se_ref, so_ref, q_ref, acc_ref, kn0, kn1, bias0, bias1, q_all):
    i = pl.program_id(0)
    half = e_ref.shape[1]

    @pl.when(i == 0)
    def _():
        fill_keys(e_ref[...], o_ref[WROWS:, :], o_ref[0:WROWS, 0:256], 0, kn0, bias0)
        fill_keys(se_ref[...], so_ref[WROWS:, :], so_ref[0:WROWS, 0:256], 0, kn1, bias1)
        factor = sharpness * LOG2E / (2 * half)
        q_all[...] = (kn0[:, : 2 * half].astype(jnp.float32) * factor).astype(jnp.bfloat16)

    q = q_all[pl.ds(pl.multiple_of(i * QB, QB), QB), :]
    q_ref[...] = q
    total = jnp.zeros(acc_ref.shape, jnp.float32)
    total = add_slab(q, kn0, bias0, total, i * QB)
    acc_ref[...] = add_slab(q, kn1, bias1, total)


def middle_kernel(flips, q_ref, acc_in, i0_ref, i1_ref, s0_ref, s1_ref, acc_ref, kn0, kn1, bias0, bias1):
    @pl.when(pl.program_id(0) == 0)
    def _():
        fill_keys(i0_ref[...], i1_ref[WROWS:, :], i1_ref[0:WROWS, 0:256], flips[0], kn0, bias0)
        fill_keys(s0_ref[...], s1_ref[WROWS:, :], s1_ref[0:WROWS, 0:256], flips[1], kn1, bias1)

    total = add_slab(q_ref[...], kn0, bias0, acc_in[...])
    acc_ref[...] = add_slab(q_ref[...], kn1, bias1, total)


def last_kernel(flips, q_ref, acc_in, d0_ref, front_ref, back_ref, out_ref, score_ref, kn0, bias0):
    i = pl.program_id(0)
    half = d0_ref.shape[1]

    @pl.when(i == 0)
    def _():
        d1 = jnp.concatenate([back_ref[...], front_ref[WROWS:, :]], axis=0)
        fill_keys(d0_ref[...], d1, front_ref[0:WROWS, 0:256], flips[1], kn0, bias0)

    total = add_slab(q_ref[...], kn0, bias0, acc_in[...])
    mass = total[:, half:]
    out_ref[...] = (total[:, :half] / jnp.concatenate([mass] * 3, axis=1)).astype(jnp.bfloat16)
    logs = jnp.log(mass) / sharpness + 1.0
    eye = lax.broadcasted_iota(jnp.int32, (128, 128), 0) == lax.broadcasted_iota(jnp.int32, (128, 128), 1)
    lines = [
        jnp.sum(jnp.where(eye, logs[b * 128 : (b + 1) * 128, :], 0.0), axis=0, keepdims=True)
        for b in range(QB // 128)
    ]
    score_ref[...] = jnp.concatenate(lines, axis=0).reshape(score_ref.shape)


def shards(embeddings, weights):
    rows, half = embeddings.shape
    count = lax.axis_size("blk")
    slab = lax.axis_index("blk")
    wide = half // 3 * 4

    def signed(step):
        pairs = []
        for to in range(count):
            source = (to + (step if to % 2 == 0 else -step)) % count
            flip = int(source // RING != to // RING)
            for r in range(2):
                pairs.append((source * 2 + r, to * 2 + (r ^ flip)))
        return pairs

    inner = signed(2)
    outer = signed(-2)
    over = lambda value, pairs: lax.ppermute(value, ("blk", "rep"), pairs)
    swap = lambda value: lax.ppermute(value, "blk", [(s, s ^ 1) for s in range(count)])
    trade = lambda value: lax.ppermute(value, "rep", [(0, 1), (1, 0)])

    sign = 1 - 2 * (slab % 2)
    wraps = lambda step: ((slab + step * sign) % count // RING != slab // RING).astype(jnp.int32)
    flips = jnp.stack([wraps(2), wraps(-2)])

    packed = jnp.full((WROWS, half), 1.0, jnp.bfloat16).at[:4, :256].set(weights.reshape(4, 256))
    other = trade(jnp.concatenate([packed, embeddings], axis=0))
    inner0 = over(embeddings, inner)
    outer0 = over(embeddings, outer)
    swapped0 = swap(embeddings)
    swapped1 = swap(other)
    inner1 = over(other, inner)
    cut = rows // 2
    outer1_front = over(jnp.concatenate([other[:WROWS], other[WROWS + cut :]], axis=0), outer)
    outer1_back = trade(outer0[:cut])
    mate0 = swap(inner0)
    mate1 = swap(inner1)

    steps = rows // QB
    whole = lambda shape: pl.BlockSpec(shape, lambda i, *_: (0,) * len(shape))
    block = lambda width: pl.BlockSpec((QB, width), lambda i, *_: (i, 0))
    keys = [pltpu.VMEM((rows, 7 * half // 3), jnp.bfloat16)]
    bias = [pltpu.VMEM((8, rows), jnp.float32)]
    params = pltpu.CompilerParams(vmem_limit_bytes=40 * 1024 * 1024, dimension_semantics=("arbitrary",))
    full0, full1 = whole((rows, half)), whole((rows + WROWS, half))

    queries, acc = pl.pallas_call(
        first_kernel,
        grid=(steps,),
        in_specs=[full0, full1, full0, full1],
        out_specs=[block(2 * half), block(wide)],
        out_shape=[
            jax.ShapeDtypeStruct((rows, 2 * half), jnp.bfloat16),
            jax.ShapeDtypeStruct((rows, wide), jnp.float32),
        ],
        scratch_shapes=keys * 2 + bias * 2 + [pltpu.VMEM((rows, 2 * half), jnp.bfloat16)],
        compiler_params=params,
        name="own_pair",
    )(embeddings, other, swapped0, swapped1)

    acc = pl.pallas_call(
        middle_kernel,
        grid_spec=pltpu.PrefetchScalarGridSpec(
            num_scalar_prefetch=1,
            grid=(steps,),
            in_specs=[block(2 * half), block(wide), full0, full1, full0, full1],
            out_specs=block(wide),
            scratch_shapes=keys * 2 + bias * 2,
        ),
        out_shape=jax.ShapeDtypeStruct((rows, wide), jnp.float32),
        compiler_params=params,
        name="inner_pair",
    )(flips, queries, acc, inner0, inner1, mate0, mate1)

    neighbours, scores = pl.pallas_call(
        last_kernel,
        grid_spec=pltpu.PrefetchScalarGridSpec(
            num_scalar_prefetch=1,
            grid=(steps,),
            in_specs=[
                block(2 * half),
                block(wide),
                full0,
                whole((rows - cut + WROWS, half)),
                whole((cut, half)),
            ],
            out_specs=[block(half), pl.BlockSpec((1, QB // 128, 128), lambda i, *_: (i, 0, 0))],
            scratch_shapes=keys + bias,
        ),
        out_shape=[
            jax.ShapeDtypeStruct((rows, half), jnp.bfloat16),
            jax.ShapeDtypeStruct((steps, QB // 128, 128), jnp.float32),
        ],
        compiler_params=params,
        name="outer_slab",
    )(flips, queries, acc, outer0, outer1_front, outer1_back)
    return neighbours, scores.reshape(rows)


def solution(mesh):
    return jax.shard_map(
        shards,
        mesh=mesh,
        in_specs=(P("blk", "rep"), P("blk")),
        out_specs=(P("blk", "rep"), P("blk")),
        check_vma=False,
    )
```

```python
import functools

import jax
import jax.numpy as jnp
from jax import lax
from jax.experimental import pallas as pl
from jax.experimental.pallas import tpu as pltpu
from jax.sharding import PartitionSpec as P
sharpness = 12.0
epsilon = 1e-06
LOG2E = 1.4426950408889634
WROWS = 16
RING = 16

def slab_kernel(*refs, sources, flip_ids, first, last, rows, half, KB, QB):
    refs = list(refs)
    flips = refs.pop(0)
    if not first:
        q_in, acc_in = refs.pop(0), refs.pop(0)
    n = len(sources)
    n_in = 1 + max(max([s["d0"], s["w"]] + [p[0] for p in s["d1"]]) for s in sources)
    ins = [refs.pop(0) for _ in range(n_in)]
    if last:
        out_ref, score_ref = refs.pop(0), refs.pop(0)
    else:
        q_out = refs.pop(0) if first else None
        acc_out = refs.pop(0)
    raw0, raw1, wt, kn, vals, q, acc, sems, qsem, asem, osem = refs
    copies = []
    for k, s in enumerate(sources):
        cs = [pltpu.make_async_copy(ins[s["d0"]], raw0.at[k], sems.at[k, 0])]
        for j, (ri, src, dst, cnt) in enumerate(s["d1"]):
            cs.append(pltpu.make_async_copy(ins[ri].at[pl.ds(src, cnt)], raw1.at[k, pl.ds(dst, cnt)], sems.at[k, 1 + j]))
        cs.append(pltpu.make_async_copy(ins[s["w"]].at[pl.ds(0, WROWS)], wt.at[k], sems.at[k, 3]))
        copies.append(cs)
    for c in copies[0]: c.start()
    if not first:
        cq = pltpu.make_async_copy(q_in, q, qsem); cq.start()
        ca = pltpu.make_async_copy(acc_in, acc, asem); ca.start()
    for cs in copies[1:]:
        for c in cs: c.start()
    wide = acc.shape[1]
    blocks = [(k, b) for k in range(n) for b in range(rows // KB)]
    eye = lax.broadcasted_iota(jnp.int32, (128, 128), 0) == lax.broadcasted_iota(jnp.int32, (128, 128), 1)

    def fill(index):
        k, b = blocks[index]
        slot = index % 2
        fid = flip_ids[k]
        for t in range(KB // 128):
            lo, r0 = t * 128, b * KB + t * 128
            line = r0 // 128
            a = raw0[k, r0:r0 + 128, :].astype(jnp.float32)
            o = raw1[k, r0:r0 + 128, :].astype(jnp.float32)
            tot = jnp.sum(a * a + o * o, axis=1, keepdims=True)
            sc = lax.rsqrt(tot / (2 * half) + epsilon)
            w_row = wt[k, 0:8, :128].astype(jnp.float32)[line:line + 1, :]
            w_col = jnp.sum(jnp.where(eye, w_row, 0.0), axis=1, keepdims=True)
            a = a * sc
            o = o * sc
            if fid is not None:
                sw = flips[fid] == 1
                a, o = jnp.where(sw, o, a), jnp.where(sw, a, o)
            kn[slot, lo:lo + 128, half:2 * half] = a.astype(jnp.bfloat16)
            kn[slot, lo:lo + 128, 0:half] = o.astype(jnp.bfloat16)
            vals[slot, lo:lo + 128, 0:half] = (a * w_col).astype(jnp.bfloat16)
            vals[slot, lo:lo + 128, half:wide] = jnp.broadcast_to(w_col, (128, wide - half)).astype(jnp.bfloat16)
            if first and k == 0:
                q[r0:r0 + 128, half:2 * half] = a.astype(jnp.bfloat16)
                q[r0:r0 + 128, 0:half] = o.astype(jnp.bfloat16)

    for c in copies[0]: c.wait()
    fill(0)
    ahead = first and len(blocks) > 1 and blocks[1][0] == 0
    if first:
        if ahead: fill(1)
    else:
        cq.wait(); ca.wait()
    waited = {0}
    nq = rows // QB
    factor = sharpness * LOG2E / (2 * half)
    for index, (k, b) in enumerate(blocks):
        if index + 1 < len(blocks) and not (ahead and index == 0):
            k2 = blocks[index + 1][0]
            if k2 not in waited:
                for c in copies[k2]: c.wait()
                waited.add(k2)
            fill(index + 1)
        slot = index % 2
        for i in range(nq):
            qs = slice(i * QB, (i + 1) * QB)
            logits = lax.dot_general(q[qs, :], kn[slot], (((1,), (1,)), ((), ())), preferred_element_type=jnp.float32)
            p = jnp.exp2(logits * factor - sharpness * LOG2E)
            if first and k == 0 and not ((i + 1) * QB <= b * KB or i * QB >= (b + 1) * KB):
                rr = lax.broadcasted_iota(jnp.int32, p.shape, 0) + i * QB
                cc = lax.broadcasted_iota(jnp.int32, p.shape, 1) + b * KB
                p = jnp.where(rr == cc, 0.0, p)
            pv = jnp.dot(p.astype(jnp.bfloat16), vals[slot], preferred_element_type=jnp.float32)
            if first and index == 0:
                acc[qs, :] = pv
            else:
                acc[qs, :] = acc[qs, :] + pv
            if index + 1 == len(blocks):
                if last:
                    for t in range(QB // 128):
                        ts = slice(i * QB + t * 128, i * QB + t * 128 + 128)
                        mass = acc[ts, half:]
                        inv = jnp.concatenate([mass] * (half // 128), axis=1)
                        out_ref[ts, :] = (acc[ts, :half] / inv).astype(jnp.bfloat16)
                        lg = jnp.log(mass) / sharpness + 1.0
                        score_ref[i * (QB // 128) + t, :] = jnp.sum(jnp.where(eye, lg, 0.0), axis=0)
                else:
                    pltpu.make_async_copy(acc.at[pl.ds(i * QB, QB)], acc_out.at[pl.ds(i * QB, QB)], osem.at[i]).start()
        if first and index == 0:
            cq = pltpu.make_async_copy(q, q_out, qsem); cq.start()
    if not last:
        for i in range(nq):
            pltpu.make_async_copy(acc.at[pl.ds(i * QB, QB)], acc_out.at[pl.ds(i * QB, QB)], osem.at[i]).wait()
    if first: cq.wait()

def slabs_call(flips, arrays, sources, flip_ids, rows, half, queries=None, acc=None, last=False, name="slabs", KB=1024, QB=512):
    first = queries is None
    n = len(sources)
    wide = half // 3 * 4
    anyspec = pl.BlockSpec(memory_space=pl.ANY)
    smem = pl.BlockSpec(memory_space=pltpu.SMEM)
    vm = pl.BlockSpec(memory_space=pltpu.VMEM)
    ops = [flips] + ([] if first else [queries, acc]) + list(arrays)
    specs = [smem] + [anyspec] * (len(ops) - 1)
    if last:
        outs = [jax.ShapeDtypeStruct((rows, half), jnp.bfloat16), jax.ShapeDtypeStruct((rows // 128, 128), jnp.float32)]
        ospecs = [vm, vm]
    else:
        outs = [jax.ShapeDtypeStruct((rows, wide), jnp.float32)]
        if first: outs = [jax.ShapeDtypeStruct((rows, 2 * half), jnp.bfloat16)] + outs
        ospecs = [anyspec] * len(outs)
    return pl.pallas_call(
        functools.partial(slab_kernel, sources=sources, first=first, last=last, rows=rows, half=half, flip_ids=flip_ids, KB=KB, QB=QB),
        in_specs=specs, out_specs=ospecs, out_shape=outs,
        scratch_shapes=[
            pltpu.VMEM((n, rows, half), jnp.bfloat16), pltpu.VMEM((n, rows, half), jnp.bfloat16),
            pltpu.VMEM((n, WROWS, half), jnp.bfloat16), pltpu.VMEM((2, KB, 2 * half), jnp.bfloat16),
            pltpu.VMEM((2, KB, wide), jnp.bfloat16),
            pltpu.VMEM((rows, 2 * half), jnp.bfloat16), pltpu.VMEM((rows, wide), jnp.float32),
            pltpu.SemaphoreType.DMA((n, 4)), pltpu.SemaphoreType.DMA, pltpu.SemaphoreType.DMA, pltpu.SemaphoreType.DMA((rows // QB,)),
        ],
        compiler_params=pltpu.CompilerParams(vmem_limit_bytes=48 * 1024 * 1024),
        name=name,
    )(*ops)


def shards(embeddings, weights):
    rows, half = embeddings.shape
    count = lax.axis_size("blk")
    slab = lax.axis_index("blk")

    def signed(step):
        pairs = []
        for to in range(count):
            source = (to + (step if to % 2 == 0 else -step)) % count
            flip = int(source // RING != to // RING)
            for r in range(2):
                pairs.append((source * 2 + r, to * 2 + (r ^ flip)))
        return pairs

    inner = signed(2)
    outer = signed(-2)
    over = lambda value, pairs: lax.ppermute(value, ("blk", "rep"), pairs)
    swap = lambda value: lax.ppermute(value, "blk", [(s, s ^ 1) for s in range(count)])
    trade = lambda value: lax.ppermute(value, "rep", [(0, 1), (1, 0)])

    sign = 1 - 2 * (slab % 2)
    wraps = lambda step: ((slab + step * sign) % count // RING != slab // RING).astype(jnp.int32)
    flips = jnp.stack([wraps(2), wraps(-2)])

    packed = jnp.full((WROWS, half), 1.0, jnp.bfloat16).at[:8, :128].set(weights.reshape(8, 128))
    inner0 = over(embeddings, inner)
    outer0 = over(embeddings, outer)
    swapped0 = swap(embeddings)
    other = trade(jnp.concatenate([packed, embeddings], axis=0))
    other, inner0, outer0, swapped0 = lax.optimization_barrier((other, inner0, outer0, swapped0))

    cut = rows // 2
    swapped1 = swap(other)
    inner1 = over(other, inner)
    mate0 = swap(inner0)
    outer1_back = trade(outer0[:cut])
    outer1_front = over(jnp.concatenate([other[:WROWS], other[WROWS + cut :]], axis=0), outer)

    whole = lambda first: {"d0": first, "d1": [(first + 1, WROWS, 0, rows)], "w": first + 1}
    queries, acc = slabs_call(
        flips, [embeddings, other, swapped0, swapped1], [whole(0), whole(2)], [None, None], rows, half, name="own_pair"
    )
    acc, inner1, outer1_back, outer1_front = lax.optimization_barrier((acc, inner1, outer1_back, outer1_front))
    mate1 = swap(inner1)
    (acc,) = slabs_call(
        flips, [inner0, inner1], [whole(0)], [0], rows, half, queries=queries, acc=acc, name="inner_slab"
    )
    halves = {"d0": 2, "d1": [(3, 0, 0, cut), (4, WROWS, cut, rows - cut)], "w": 4}
    neighbours, scores = slabs_call(
        flips,
        [mate0, mate1, outer0, outer1_back, outer1_front],
        [whole(0), halves],
        [1, 1],
        rows,
        half,
        queries=queries,
        acc=acc,
        last=True,
        name="last_pair",
    )
    return neighbours, scores.reshape(rows)


def solution(mesh):
    return jax.shard_map(
        shards,
        mesh=mesh,
        in_specs=(P("blk", "rep"), P("blk")),
        out_specs=(P("blk", "rep"), P("blk")),
        check_vma=False,
    )
```

```python
import functools

import jax
import jax.numpy as jnp
from jax import lax
from jax.experimental import pallas as pl
from jax.experimental.pallas import tpu as pltpu
from jax.sharding import PartitionSpec as P
sharpness = 12.0
epsilon = 1e-06
LOG2E = 1.4426950408889634
WROWS = 16
RING = 16

def slab_kernel(*refs, sources, flip_ids, first, last, rows, half, KB, QB):
    refs = list(refs)
    flips = refs.pop(0)
    if not first:
        q_in, acc_in = refs.pop(0), refs.pop(0)
    n = len(sources)
    n_in = 1 + max(max([s["d0"], s["w"]] + [p[0] for p in s["d1"]]) for s in sources)
    ins = [refs.pop(0) for _ in range(n_in)]
    if last:
        out_ref, score_ref = refs.pop(0), refs.pop(0)
    else:
        q_out = refs.pop(0) if first else None
        acc_out = refs.pop(0)
    raw0, raw1, wt, kn, vals, q, acc, old, sems, qsem, asem, osem = refs
    copies = []
    for k, s in enumerate(sources):
        cs = [pltpu.make_async_copy(ins[s["d0"]], raw0.at[k], sems.at[k, 0])]
        for j, (ri, src, dst, cnt) in enumerate(s["d1"]):
            cs.append(pltpu.make_async_copy(ins[ri].at[pl.ds(src, cnt)], raw1.at[k, pl.ds(dst, cnt)], sems.at[k, 1 + j]))
        cs.append(pltpu.make_async_copy(ins[s["w"]].at[pl.ds(0, WROWS)], wt.at[k], sems.at[k, 3]))
        copies.append(cs)
    for c in copies[0]: c.start()
    if not first:
        cq = pltpu.make_async_copy(q_in, q, qsem); cq.start()
        ca = pltpu.make_async_copy(acc_in, old, asem)
    for cs in copies[1:]:
        for c in cs: c.start()
    if not first:
        ca.start()
    wide = acc.shape[1]
    blocks = [(k, b) for k in range(n) for b in range(rows // KB)]
    eye = lax.broadcasted_iota(jnp.int32, (128, 128), 0) == lax.broadcasted_iota(jnp.int32, (128, 128), 1)

    def fill(index):
        k, b = blocks[index]
        slot = index % 2
        fid = flip_ids[k]
        for t in range(KB // 128):
            lo, r0 = t * 128, b * KB + t * 128
            line = r0 // 128
            a = raw0[k, r0:r0 + 128, :].astype(jnp.float32)
            o = raw1[k, r0:r0 + 128, :].astype(jnp.float32)
            tot = jnp.sum(a * a + o * o, axis=1, keepdims=True)
            sc = lax.rsqrt(tot / (2 * half) + epsilon)
            w_row = wt[k, 0:8, :128].astype(jnp.float32)[line:line + 1, :]
            w_col = jnp.sum(jnp.where(eye, w_row, 0.0), axis=1, keepdims=True)
            a = a * sc
            o = o * sc
            if fid is not None:
                sw = flips[fid] == 1
                a, o = jnp.where(sw, o, a), jnp.where(sw, a, o)
            kn[slot, lo:lo + 128, half:2 * half] = a.astype(jnp.bfloat16)
            kn[slot, lo:lo + 128, 0:half] = o.astype(jnp.bfloat16)
            vals[slot, lo:lo + 128, 0:half] = (a * w_col).astype(jnp.bfloat16)
            vals[slot, lo:lo + 128, half:wide] = jnp.broadcast_to(w_col, (128, wide - half)).astype(jnp.bfloat16)
            if first and k == 0:
                q[r0:r0 + 128, half:2 * half] = a.astype(jnp.bfloat16)
                q[r0:r0 + 128, 0:half] = o.astype(jnp.bfloat16)

    for c in copies[0]: c.wait()
    fill(0)
    ahead = first and len(blocks) > 1 and blocks[1][0] == 0
    if first:
        if ahead: fill(1)
    else:
        cq.wait()
    waited = {0}
    nq = rows // QB
    factor = sharpness * LOG2E / (2 * half)
    for index, (k, b) in enumerate(blocks):
        if index + 1 < len(blocks) and not (ahead and index == 0):
            k2 = blocks[index + 1][0]
            if k2 not in waited:
                for c in copies[k2]: c.wait()
                waited.add(k2)
            fill(index + 1)
        slot = index % 2
        for i in range(nq):
            qs = slice(i * QB, (i + 1) * QB)
            logits = lax.dot_general(q[qs, :], kn[slot], (((1,), (1,)), ((), ())), preferred_element_type=jnp.float32)
            p = jnp.exp2(logits * factor - sharpness * LOG2E)
            if first and k == 0 and not ((i + 1) * QB <= b * KB or i * QB >= (b + 1) * KB):
                rr = lax.broadcasted_iota(jnp.int32, p.shape, 0) + i * QB
                cc = lax.broadcasted_iota(jnp.int32, p.shape, 1) + b * KB
                p = jnp.where(rr == cc, 0.0, p)
            pv = jnp.dot(p.astype(jnp.bfloat16), vals[slot], preferred_element_type=jnp.float32)
            if index == 0:
                acc[qs, :] = pv
            elif index + 1 < len(blocks) or first:
                acc[qs, :] = acc[qs, :] + pv
            else:
                if i == 0:
                    ca.wait()
                acc[qs, :] = acc[qs, :] + pv + old[qs, :]
            if index == 0 and len(blocks) == 1 and not first:
                if i == 0:
                    ca.wait()
                acc[qs, :] = acc[qs, :] + old[qs, :]
            if index + 1 == len(blocks):
                if last:
                    for t in range(QB // 128):
                        ts = slice(i * QB + t * 128, i * QB + t * 128 + 128)
                        mass = acc[ts, half:]
                        inv = jnp.concatenate([mass] * (half // 128), axis=1)
                        out_ref[ts, :] = (acc[ts, :half] / inv).astype(jnp.bfloat16)
                        lg = jnp.log(mass) / sharpness + 1.0
                        score_ref[i * (QB // 128) + t, :] = jnp.sum(jnp.where(eye, lg, 0.0), axis=0)
                else:
                    pltpu.make_async_copy(acc.at[pl.ds(i * QB, QB)], acc_out.at[pl.ds(i * QB, QB)], osem.at[i]).start()
        if first and index == 0:
            cq = pltpu.make_async_copy(q, q_out, qsem); cq.start()
    if not last:
        for i in range(nq):
            pltpu.make_async_copy(acc.at[pl.ds(i * QB, QB)], acc_out.at[pl.ds(i * QB, QB)], osem.at[i]).wait()
    if first: cq.wait()

def slabs_call(flips, arrays, sources, flip_ids, rows, half, queries=None, acc=None, last=False, name="slabs", KB=1024, QB=512):
    first = queries is None
    n = len(sources)
    wide = half // 3 * 4
    anyspec = pl.BlockSpec(memory_space=pl.ANY)
    smem = pl.BlockSpec(memory_space=pltpu.SMEM)
    vm = pl.BlockSpec(memory_space=pltpu.VMEM)
    ops = [flips] + ([] if first else [queries, acc]) + list(arrays)
    specs = [smem] + [anyspec] * (len(ops) - 1)
    if last:
        outs = [jax.ShapeDtypeStruct((rows, half), jnp.bfloat16), jax.ShapeDtypeStruct((rows // 128, 128), jnp.float32)]
        ospecs = [vm, vm]
    else:
        outs = [jax.ShapeDtypeStruct((rows, wide), jnp.float32)]
        if first: outs = [jax.ShapeDtypeStruct((rows, 2 * half), jnp.bfloat16)] + outs
        ospecs = [anyspec] * len(outs)
    return pl.pallas_call(
        functools.partial(slab_kernel, sources=sources, first=first, last=last, rows=rows, half=half, flip_ids=flip_ids, KB=KB, QB=QB),
        in_specs=specs, out_specs=ospecs, out_shape=outs,
        scratch_shapes=[
            pltpu.VMEM((n, rows, half), jnp.bfloat16), pltpu.VMEM((n, rows, half), jnp.bfloat16),
            pltpu.VMEM((n, WROWS, 128), jnp.bfloat16), pltpu.VMEM((2, KB, 2 * half), jnp.bfloat16),
            pltpu.VMEM((2, KB, wide), jnp.bfloat16),
            pltpu.VMEM((rows, 2 * half), jnp.bfloat16), pltpu.VMEM((rows, wide), jnp.float32), pltpu.VMEM((8 if first else rows, wide), jnp.float32),
            pltpu.SemaphoreType.DMA((n, 4)), pltpu.SemaphoreType.DMA, pltpu.SemaphoreType.DMA, pltpu.SemaphoreType.DMA((rows // QB,)),
        ],
        compiler_params=pltpu.CompilerParams(vmem_limit_bytes=28 * 1024 * 1024),
        name=name,
    )(*ops)


def shards(embeddings, weights):
    rows, half = embeddings.shape
    count = lax.axis_size("blk")
    slab = lax.axis_index("blk")

    def signed(step):
        pairs = []
        for to in range(count):
            source = (to + (step if to % 2 == 0 else -step)) % count
            flip = int(source // RING != to // RING)
            for r in range(2):
                pairs.append((source * 2 + r, to * 2 + (r ^ flip)))
        return pairs

    inner = signed(2)
    outer = signed(-2)
    over = lambda value, pairs: lax.ppermute(value, ("blk", "rep"), pairs)
    swap = lambda value: lax.ppermute(value, "blk", [(s, s ^ 1) for s in range(count)])
    trade = lambda value: lax.ppermute(value, "rep", [(0, 1), (1, 0)])

    sign = 1 - 2 * (slab % 2)
    wraps = lambda step: ((slab + step * sign) % count // RING != slab // RING).astype(jnp.int32)
    flips = jnp.stack([wraps(2), wraps(-2)])

    lines = weights.reshape(rows // 128, 128)
    own_w = jnp.concatenate([lines] * (WROWS * 128 // rows), axis=0)
    inner0 = over(embeddings, inner)
    outer0 = over(embeddings, outer)
    other = trade(embeddings)
    inner_w = over(own_w, inner)
    outer_w = over(own_w, outer)
    other, inner0, outer0, inner_w, outer_w = lax.optimization_barrier(
        (other, inner0, outer0, inner_w, outer_w)
    )

    inner1 = over(other, inner)
    swapped1 = swap(other)
    swapped0 = swap(embeddings)
    swapped_w = swap(own_w)
    mate0 = swap(inner0)
    mate_w = swap(inner_w)
    outer1 = trade(outer0)

    whole = lambda first: {"d0": first, "d1": [(first + 1, 0, 0, rows)], "w": first + 2}
    queries, acc = slabs_call(
        flips, [embeddings, other, own_w, swapped0, swapped1, swapped_w],
        [whole(0), whole(3)], [None, None], rows, half, name="own_pair"
    )
    acc, inner1, outer1 = lax.optimization_barrier((acc, inner1, outer1))
    mate1 = swap(inner1)
    outer_slab = {"d0": 6, "d1": [(7, 0, 0, rows)], "w": 8}
    neighbours, scores = slabs_call(
        flips,
        [inner0, inner1, inner_w, mate0, mate1, mate_w, outer0, outer1, outer_w],
        [whole(0), whole(3), outer_slab],
        [0, 1, 1],
        rows,
        half,
        queries=queries,
        acc=acc,
        last=True,
        name="last_three",
    )
    return neighbours, scores.reshape(rows)


def solution(mesh):
    return jax.shard_map(
        shards,
        mesh=mesh,
        in_specs=(P("blk", "rep"), P("blk")),
        out_specs=(P("blk", "rep"), P("blk")),
        check_vma=False,
    )
```
